32 devices in a mesh: bin: 8 (over y, x, core), dp: 4 (over z).
Axes of the slice: x: 2, y: 2, z: 4, core: 2. Of those that a mesh axis runs over, the one named last changes fastest.
Arguments:
- peak_bins: int32 [512, 128], P('dp'), may hold values from 0 to 196607
- peak_values: bfloat16 [512, 128], P('dp'), may hold values from 0.049804688 to 1
- enc_weight: bfloat16 [196608, 2048], P(('bin', 'dp')), may hold values from -0.5 to 0.5
- enc_bias: float32 [2048], replicated, may hold values from -3 to 3
- dec_weight: bfloat16 [2048, 196608], P(None, ('bin', 'dp')), may hold values from -0.0007324219 to 0.0007324219
Outputs:
- grad_enc: bfloat16 [196608, 2048], P(('bin', 'dp'))
- grad_dec: bfloat16 [2048, 196608], P(None, ('bin', 'dp'))
The draws below stay inside these ranges and needn't reach their ends.
All inputs are finite; a program needn't handle non-finite values.
Results may differ from the reference program's by a relative error of at most 0.0057.
Values may be sent and summed in bfloat16 or wider, within the bound.
A program may use at most 192 MiB of HBM per device.

```python
import math
import jax
import jax.numpy as jnp

BINS = 196608
HIDDEN_SIZE = 2048
PEAKS = 128
SPECTRA = 512


def plant(values, rng, smallest, top_value):
    place = [jax.random.randint(jax.random.fold_in(rng, axis), (), 0, length) for axis, length in enumerate(values.shape)]
    widest = values.shape.index(max(values.shape))
    neighbour = place[:widest] + [(place[widest] + 1) % values.shape[widest]] + place[widest + 1:]
    return values.at[tuple(place)].set(smallest).at[tuple(neighbour)].set(top_value)


def steps_of(key, shape, shards, low, largest):
    gain, own = 1.0, jax.random.fold_in(key, 6)
    for position, shards_of in shards:
        heights = jnp.exp(jax.random.uniform(jax.random.fold_in(own, position), (shards_of,), jnp.float32, low / len(shards), largest / len(shards)))
        gain = gain * jnp.repeat(heights, shape[position] // shards_of).reshape([-1 if axis == position else 1 for axis in range(len(shape))])
    return gain


def bell_draw(key, shape, deviation, limit, cuts=(), kind=jnp.bfloat16):
    array = jax.random.normal(key, shape, jnp.float32) * deviation
    if len(cuts) > 0:
        array = steps_of(key, shape, cuts, -0.22, 0.18) * array
    return jnp.clip(array, min=-limit, max=limit).astype(kind)


def setup_inputs(seed: int = 0) -> dict:
    streams_of = jax.random.split(jax.random.key(seed), 6)
    peak_bins = plant(jax.random.randint(streams_of[0], (SPECTRA, PEAKS), 0, BINS), jax.random.fold_in(streams_of[0], 1), 0, BINS - 1).astype(jnp.int32)
    peak_values = jnp.clip(jnp.exp(math.log(1.0) - 2.9996462 * jax.random.uniform(streams_of[1], (SPECTRA, PEAKS), jnp.float32) ** steps_of(streams_of[1], (SPECTRA, PEAKS), ((0, 4),), -0.2, 0.2)), 0.049804688, 1.0).astype(jnp.bfloat16)
    enc_weight = bell_draw(streams_of[2], (BINS, HIDDEN_SIZE), PEAKS ** -0.5, 0.5, ((0, 32),))
    enc_bias = bell_draw(streams_of[3], (HIDDEN_SIZE,), 0.5, 3.0, (), jnp.float32)
    dec_weight = bell_draw(streams_of[4], (HIDDEN_SIZE, BINS), (2.0 * PEAKS ** 0.5 / BINS), 0.0007324219, ((1, 32),))
    return {"peak_bins": peak_bins, "peak_values": peak_values, "enc_weight": enc_weight, "enc_bias": enc_bias, "dec_weight": dec_weight}


def activation(values):
    return jax.nn.gelu(values, approximate=True)

def reference(peak_bins, peak_values, enc_weight, enc_bias, dec_weight):
    row_ids = jnp.broadcast_to(jnp.arange(SPECTRA, dtype=jnp.int32)[:, None], peak_bins.shape)
    dense = jnp.zeros((SPECTRA, BINS), jnp.float32).at[row_ids, peak_bins].add(peak_values.astype(jnp.float32)).astype(jnp.bfloat16)
    pre = jnp.dot(dense, enc_weight, preferred_element_type=jnp.float32) + enc_bias
    hidden = activation(pre).astype(jnp.bfloat16)
    recon = jnp.dot(hidden, dec_weight, preferred_element_type=jnp.float32)
    resid = (recon - dense.astype(jnp.float32)).astype(jnp.bfloat16)
    grad_dec = jnp.dot(hidden.T, resid, preferred_element_type=jnp.float32).astype(jnp.bfloat16)
    back = jnp.dot(resid, dec_weight.T, preferred_element_type=jnp.float32)
    _, pullback = jax.vjp(activation, pre)
    dpre = pullback(back)[0].astype(jnp.bfloat16)
    grad_enc = jnp.dot(dense.T, dpre, preferred_element_type=jnp.float32).astype(jnp.bfloat16)
    return (grad_enc, grad_dec)
```

```python
import functools

import jax
import jax.numpy as jnp
from jax import lax
from jax.experimental import pallas as pl
from jax.experimental.pallas import tpu as pltpu
from jax.sharding import PartitionSpec as P

AXES = ("bin", "dp")
LOW = 256
GROUP = 8


def activation(values):
    return jax.nn.gelu(values, approximate=True)


def slope_times(pre, back):
    _, pullback = jax.vjp(activation, pre)
    return pullback(back)[0].astype(jnp.bfloat16)


def spread_kernel(highs, bins_ref, values_ref, dense_ref):
    rows = GROUP * highs
    row_ids = lax.broadcasted_iota(jnp.int32, (rows, 128), 0)
    low_ids = lax.broadcasted_iota(jnp.int32, (LOW, 128), 0)
    sums = []
    for half in range(2):
        total = jnp.zeros((rows, LOW), jnp.float32)
        picks, lows = [], []
        for s in range(GROUP):
            row = half * GROUP + s
            local = bins_ref[row : row + 1, :]
            value = values_ref[row : row + 1, :]
            high = jnp.where(local < 0, -1, lax.shift_right_arithmetic(local, 8))
            key = jnp.where(high < 0, -1, high * GROUP + s)
            low = lax.bitwise_and(local, LOW - 1)
            picks.append(jnp.where(row_ids == key, value, 0.0).astype(jnp.bfloat16))
            lows.append(jnp.where(low_ids == low, 1.0, 0.0).astype(jnp.bfloat16))
        sums.append(
            lax.dot_general(
                jnp.concatenate(picks, axis=1),
                jnp.concatenate(lows, axis=1),
                (((1,), (1,)), ((), ())),
                preferred_element_type=jnp.float32,
            )
        )
    for high in range(highs):
        part = slice(high * GROUP, (high + 1) * GROUP)
        dense_ref[:, high * LOW : (high + 1) * LOW] = jnp.concatenate(
            [sums[0][part], sums[1][part]], axis=0
        ).astype(jnp.bfloat16)


def spread(local_bins, values, bins_dev):
    rows, peaks = local_bins.shape
    return pl.pallas_call(
        functools.partial(spread_kernel, bins_dev // LOW),
        grid=(rows // (2 * GROUP),),
        out_shape=jax.ShapeDtypeStruct((rows, bins_dev), jnp.bfloat16),
        in_specs=[pl.BlockSpec((2 * GROUP, peaks), lambda i: (i, 0))] * 2,
        out_specs=pl.BlockSpec((2 * GROUP, bins_dev), lambda i: (i, 0)),
        compiler_params=pltpu.CompilerParams(vmem_limit_bytes=32 * 2**20),
    )(local_bins, values)


def on_device(peak_bins, peak_values, enc_weight, enc_bias, dec_weight):
    bins_dev = enc_weight.shape[0]
    first_bin = (lax.axis_index("bin") * lax.axis_size("dp") + lax.axis_index("dp")) * bins_dev
    both = jnp.stack([peak_bins.astype(jnp.float32), peak_values.astype(jnp.float32)])
    both = lax.all_gather(both, "dp", axis=1, tiled=True)
    dense = spread(both[0].astype(jnp.int32) - first_bin, both[1], bins_dev)
    partial_pre = jnp.dot(dense, enc_weight, preferred_element_type=jnp.float32)
    own_pre = lax.psum_scatter(partial_pre, AXES, scatter_dimension=0, tiled=True) + enc_bias
    hidden = lax.all_gather(activation(own_pre).astype(jnp.bfloat16), AXES, axis=0, tiled=True)
    recon = jnp.dot(hidden, dec_weight, preferred_element_type=jnp.float32)
    resid = (recon - dense.astype(jnp.float32)).astype(jnp.bfloat16)
    partial_back = lax.dot_general(
        resid, dec_weight, (((1,), (1,)), ((), ())), preferred_element_type=jnp.float32
    )
    own_back = lax.psum_scatter(partial_back, AXES, scatter_dimension=0, tiled=True)
    grad_dec = lax.dot_general(
        hidden, resid, (((0,), (0,)), ((), ())), preferred_element_type=jnp.float32
    ).astype(jnp.bfloat16)
    dpre = lax.all_gather(slope_times(own_pre, own_back), AXES, axis=0, tiled=True)
    grad_enc = lax.dot_general(
        dense, dpre, (((0,), (0,)), ((), ())), preferred_element_type=jnp.float32
    ).astype(jnp.bfloat16)
    return (grad_enc, grad_dec)


def solution(mesh):
    placed = (P("dp", None), P("dp", None), P(AXES, None), P(), P(None, AXES))
    return jax.shard_map(
        on_device,
        mesh=mesh,
        in_specs=placed,
        out_specs=(P(AXES, None), P(None, AXES)),
        check_vma=False,
    )
```

```python
import functools

import jax
import jax.numpy as jnp
from jax import lax
from jax.experimental import pallas as pl
from jax.experimental.pallas import tpu as pltpu
from jax.sharding import PartitionSpec as P

AXES = ("bin", "dp")
LOW = 256
GROUP = 8


def activation(values):
    return jax.nn.gelu(values, approximate=True)


def slope_times(pre, back):
    _, pullback = jax.vjp(activation, pre)
    return pullback(back)[0].astype(jnp.bfloat16)


def spread_kernel(highs, bins_ref, values_ref, dense_ref):
    rows = GROUP * highs
    row_ids = lax.broadcasted_iota(jnp.int32, (rows, 128), 0)
    low_ids = lax.broadcasted_iota(jnp.int32, (LOW, 128), 0)
    sums = []
    for half in range(2):
        total = jnp.zeros((rows, LOW), jnp.float32)
        picks, lows = [], []
        for s in range(GROUP):
            row = half * GROUP + s
            local = bins_ref[row : row + 1, :]
            value = values_ref[row : row + 1, :]
            high = jnp.where(local < 0, -1, lax.shift_right_arithmetic(local, 8))
            key = jnp.where(high < 0, -1, high * GROUP + s)
            low = lax.bitwise_and(local, LOW - 1)
            picks.append(jnp.where(row_ids == key, value, 0.0).astype(jnp.bfloat16))
            lows.append(jnp.where(low_ids == low, 1.0, 0.0).astype(jnp.bfloat16))
        sums.append(
            lax.dot_general(
                jnp.concatenate(picks, axis=1),
                jnp.concatenate(lows, axis=1),
                (((1,), (1,)), ((), ())),
                preferred_element_type=jnp.float32,
            )
        )
    for high in range(highs):
        part = slice(high * GROUP, (high + 1) * GROUP)
        dense_ref[:, high * LOW : (high + 1) * LOW] = jnp.concatenate(
            [sums[0][part], sums[1][part]], axis=0
        ).astype(jnp.bfloat16)


def spread(local_bins, values, bins_dev):
    rows, peaks = local_bins.shape
    return pl.pallas_call(
        functools.partial(spread_kernel, bins_dev // LOW),
        grid=(rows // (2 * GROUP),),
        out_shape=jax.ShapeDtypeStruct((rows, bins_dev), jnp.bfloat16),
        in_specs=[pl.BlockSpec((2 * GROUP, peaks), lambda i: (i, 0))] * 2,
        out_specs=pl.BlockSpec((2 * GROUP, bins_dev), lambda i: (i, 0)),
        compiler_params=pltpu.CompilerParams(vmem_limit_bytes=32 * 2**20),
    )(local_bins, values)


def stages(part):
    bits = {name: lax.axis_size(name).bit_length() - 1 for name in AXES}
    others = list(range(1, bits["bin"]))
    if part:
        others = others[::-1]
    return (
        [("bin", bit) for bit in [0] + others] + [("dp", bit) for bit in range(bits["dp"])]
    )


def swap(values, name, bit):
    pairs = [(i, i ^ (1 << bit)) for i in range(lax.axis_size(name))]
    return lax.ppermute(values, name, pairs)


def bit_of(name, bit):
    return lax.bitwise_and(lax.shift_right_logical(lax.axis_index(name), bit), 1)


def scatter_sum(values, part, narrow):
    for name, bit in stages(part):
        half = values.shape[0] // 2
        mine = bit_of(name, bit)
        keep = lax.dynamic_slice_in_dim(values, mine * half, half, 0)
        send = lax.dynamic_slice_in_dim(values, (1 - mine) * half, half, 0)
        if narrow and name == "bin" and bit > 0:
            send = send.astype(jnp.bfloat16)
        values = keep + swap(send, name, bit).astype(jnp.float32)
    return values


def gather(values, part):
    for name, bit in stages(part)[::-1]:
        theirs = swap(values, name, bit)
        values = jnp.where(
            bit_of(name, bit) == 0,
            jnp.concatenate([values, theirs], axis=0),
            jnp.concatenate([theirs, values], axis=0),
        )
    return values


def on_device(peak_bins, peak_values, enc_weight, enc_bias, dec_weight):
    bins_dev = enc_weight.shape[0]
    first_bin = (lax.axis_index("bin") * lax.axis_size("dp") + lax.axis_index("dp")) * bins_dev
    both = jnp.stack([peak_bins.astype(jnp.float32), peak_values.astype(jnp.float32)])
    both = lax.all_gather(both, "dp", axis=1, tiled=True)
    dense = spread(both[0].astype(jnp.int32) - first_bin, both[1], bins_dev)
    rows = dense.shape[0] // 2
    parts = (0, 1)
    dense_of = [dense[part * rows : (part + 1) * rows] for part in parts]
    partial_pre = [
        jnp.dot(dense_of[part], enc_weight, preferred_element_type=jnp.float32) for part in parts
    ]
    own_pre = [scatter_sum(partial_pre[part], part, False) + enc_bias for part in parts]
    hidden_of = [gather(activation(own_pre[part]).astype(jnp.bfloat16), part) for part in parts]
    resid_of, own_back = [], []
    for part in parts:
        recon = jnp.dot(hidden_of[part], dec_weight, preferred_element_type=jnp.float32)
        resid = (recon - dense_of[part].astype(jnp.float32)).astype(jnp.bfloat16)
        partial_back = lax.dot_general(
            resid, dec_weight, (((1,), (1,)), ((), ())), preferred_element_type=jnp.float32
        )
        resid_of.append(resid)
        own_back.append(scatter_sum(partial_back, part, True))
    hidden = jnp.concatenate(hidden_of, axis=0)
    resid = jnp.concatenate(resid_of, axis=0)
    grad_dec = lax.dot_general(
        hidden, resid, (((0,), (0,)), ((), ())), preferred_element_type=jnp.float32
    ).astype(jnp.bfloat16)
    dpre = jnp.concatenate(
        [gather(slope_times(own_pre[part], own_back[part]), part) for part in parts], axis=0
    )
    grad_enc = lax.dot_general(
        dense, dpre, (((0,), (0,)), ((), ())), preferred_element_type=jnp.float32
    ).astype(jnp.bfloat16)
    return (grad_enc, grad_dec)


def solution(mesh):
    placed = (P("dp", None), P("dp", None), P(AXES, None), P(), P(None, AXES))
    return jax.shard_map(
        on_device,
        mesh=mesh,
        in_specs=placed,
        out_specs=(P(AXES, None), P(None, AXES)),
        check_vma=False,
    )
```

```python
import functools

import jax
import jax.numpy as jnp
from jax import lax
from jax.experimental import pallas as pl
from jax.experimental.pallas import tpu as pltpu
from jax.sharding import PartitionSpec as P

AXES = ("bin", "dp")
LOW = 256
GROUP = 8


def activation(values):
    return jax.nn.gelu(values, approximate=True)


def slope_times(pre, back):
    _, pullback = jax.vjp(activation, pre)
    return pullback(back)[0].astype(jnp.bfloat16)


def spread_kernel(highs, bins_ref, values_ref, dense_ref):
    rows = GROUP * highs
    row_ids = lax.broadcasted_iota(jnp.int32, (rows, 128), 0)
    low_ids = lax.broadcasted_iota(jnp.int32, (LOW, 128), 0)
    sums = []
    for half in range(2):
        total = jnp.zeros((rows, LOW), jnp.float32)
        picks, lows = [], []
        for s in range(GROUP):
            row = half * GROUP + s
            local = bins_ref[row : row + 1, :]
            value = values_ref[row : row + 1, :]
            high = jnp.where(local < 0, -1, lax.shift_right_arithmetic(local, 8))
            key = jnp.where(high < 0, -1, high * GROUP + s)
            low = lax.bitwise_and(local, LOW - 1)
            picks.append(jnp.where(row_ids == key, value, 0.0).astype(jnp.bfloat16))
            lows.append(jnp.where(low_ids == low, 1.0, 0.0).astype(jnp.bfloat16))
        sums.append(
            lax.dot_general(
                jnp.concatenate(picks, axis=1),
                jnp.concatenate(lows, axis=1),
                (((1,), (1,)), ((), ())),
                preferred_element_type=jnp.float32,
            )
        )
    for high in range(highs):
        part = slice(high * GROUP, (high + 1) * GROUP)
        dense_ref[:, high * LOW : (high + 1) * LOW] = jnp.concatenate(
            [sums[0][part], sums[1][part]], axis=0
        ).astype(jnp.bfloat16)


def spread(local_bins, values, bins_dev):
    rows, peaks = local_bins.shape
    return pl.pallas_call(
        functools.partial(spread_kernel, bins_dev // LOW),
        grid=(rows // (2 * GROUP),),
        out_shape=jax.ShapeDtypeStruct((rows, bins_dev), jnp.bfloat16),
        in_specs=[pl.BlockSpec((2 * GROUP, peaks), lambda i: (i, 0))] * 2,
        out_specs=pl.BlockSpec((2 * GROUP, bins_dev), lambda i: (i, 0)),
        compiler_params=pltpu.CompilerParams(vmem_limit_bytes=32 * 2**20),
    )(local_bins, values)


def stages(part):
    bits = {name: lax.axis_size(name).bit_length() - 1 for name in AXES}
    others = list(range(1, bits["bin"]))
    if part:
        others = others[::-1]
    return (
        [("bin", bit) for bit in [0] + others] + [("dp", bit) for bit in range(bits["dp"])]
    )


def swap(values, name, bit):
    pairs = [(i, i ^ (1 << bit)) for i in range(lax.axis_size(name))]
    return lax.ppermute(values, name, pairs)


def bit_of(name, bit):
    return lax.bitwise_and(lax.shift_right_logical(lax.axis_index(name), bit), 1)


def scatter_sum(values, part, narrow_axes):
    for name, bit in stages(part):
        half = values.shape[0] // 2
        mine = bit_of(name, bit)
        keep = lax.dynamic_slice_in_dim(values, mine * half, half, 0)
        send = lax.dynamic_slice_in_dim(values, (1 - mine) * half, half, 0)
        if name in narrow_axes and (name, bit) != ("bin", 0):
            send = send.astype(jnp.bfloat16)
        values = keep + swap(send, name, bit).astype(jnp.float32)
    return values


def gather(values, part):
    for name, bit in stages(part)[::-1]:
        theirs = swap(values, name, bit)
        values = jnp.where(
            bit_of(name, bit) == 0,
            jnp.concatenate([values, theirs], axis=0),
            jnp.concatenate([theirs, values], axis=0),
        )
    return values


def on_device(peak_bins, peak_values, enc_weight, enc_bias, dec_weight):
    bins_dev = enc_weight.shape[0]
    first_bin = (lax.axis_index("bin") * lax.axis_size("dp") + lax.axis_index("dp")) * bins_dev
    both = jnp.stack([peak_bins.astype(jnp.float32), peak_values.astype(jnp.float32)])
    both = lax.all_gather(both, "dp", axis=1, tiled=True)
    dense = spread(both[0].astype(jnp.int32) - first_bin, both[1], bins_dev)
    rows = dense.shape[0] // 2
    parts = (0, 1)
    dense_of = [dense[part * rows : (part + 1) * rows] for part in parts]
    partial_pre = [
        jnp.dot(dense_of[part], enc_weight, preferred_element_type=jnp.float32) for part in parts
    ]
    own_pre = [scatter_sum(partial_pre[part], part, ("bin",)) + enc_bias for part in parts]
    hidden_of = [gather(activation(own_pre[part]).astype(jnp.bfloat16), part) for part in parts]
    resid_of, own_back = [], []
    for part in parts:
        recon = jnp.dot(hidden_of[part], dec_weight, preferred_element_type=jnp.float32)
        resid = (recon - dense_of[part].astype(jnp.float32)).astype(jnp.bfloat16)
        partial_back = lax.dot_general(
            resid, dec_weight, (((1,), (1,)), ((), ())), preferred_element_type=jnp.float32
        )
        resid_of.append(resid)
        own_back.append(scatter_sum(partial_back, part, AXES))
    hidden = jnp.concatenate(hidden_of, axis=0)
    resid = jnp.concatenate(resid_of, axis=0)
    grad_dec = lax.dot_general(
        hidden, resid, (((0,), (0,)), ((), ())), preferred_element_type=jnp.float32
    ).astype(jnp.bfloat16)
    dpre = jnp.concatenate(
        [gather(slope_times(own_pre[part], own_back[part]), part) for part in parts], axis=0
    )
    grad_enc = lax.dot_general(
        dense, dpre, (((0,), (0,)), ((), ())), preferred_element_type=jnp.float32
    ).astype(jnp.bfloat16)
    return (grad_enc, grad_dec)


def solution(mesh):
    placed = (P("dp", None), P("dp", None), P(AXES, None), P(), P(None, AXES))
    return jax.shard_map(
        on_device,
        mesh=mesh,
        in_specs=placed,
        out_specs=(P(AXES, None), P(None, AXES)),
        check_vma=False,
    )
```
